256 devices in a mesh: tp: 8 (over y, core), ad: 32 (over x, z).
Axes of the slice: x: 4, y: 4, z: 8, core: 2. Of those that a mesh axis runs over, the one named last changes fastest.
Arguments:
- hidden: bfloat16 [8192, 8192], P('ad'), may hold values from -6 to 6
- key_value_weight: bfloat16 [8192, 2048], P(None, 'tp'), may hold values from -0.0625 to 0.0625
- request_group: int32 [8192, 1], P('ad'), may hold values from 0 to 31; in each aligned block of 256 rows (0 to 255, 256 to 511, ...) at most 16 rows name the same one
- request_member: int32 [8192], P('ad'), may hold values from 0 to 3
- adapter_down_weight: bfloat16 [8192, 8192], P('tp', 'ad'), may hold values from -0.0625 to 0.0625
- adapter_up_weight: bfloat16 [8192, 2048], P('ad', 'tp'), may hold values from -0.75 to 0.75
Outputs:
- kv_out: bfloat16 [8192, 2048], P('ad', 'tp')
The draws below stay inside these ranges and needn't reach their ends.
Inputs may be any that keep to these rules, and one draw needn't show every extreme that they name: `request_group`: among the 256 rows of one index of ad, no group is named by more than 16 rows, a bound that some block reaches.
All inputs are finite; a program needn't handle non-finite values.
Results may differ from the reference program's by a relative error of at most 0.007.
Values may be sent and summed in bfloat16 or wider, within the bound.
A program may use at most 128 MiB of HBM per device.

```python
import math
import jax
import jax.numpy as jnp
import numpy as np
from jax import lax

MODEL_WIDTH = 8192
KEY_VALUE_WIDTH = 1024
ADAPTER_RANK = 64
ADP_DEV = 4
ROWS_DEV = 256
ADAPTER_COUNT = 128
REQUEST_COUNT = 8192
CAP = 16
N_AD = 32


def plant(result, rng, low, high):
    index_at = [jax.random.randint(jax.random.fold_in(rng, axis), (), 0, length) for axis, length in enumerate(result.shape)]
    widest = result.shape.index(max(result.shape))
    next_to = index_at[:widest] + [(index_at[widest] + 1) % result.shape[widest]] + index_at[widest + 1:]
    return result.at[tuple(index_at)].set(low).at[tuple(next_to)].set(high)


def steps_of(rng, shape, cuts, low, high):
    level = 1.0
    for axis_at, blocks in cuts:
        draws = jax.random.uniform(jax.random.fold_in(jax.random.fold_in(rng, 6), axis_at), (blocks,), jnp.float32, low / len(cuts), high / len(cuts))
        level = level * jnp.repeat(jnp.exp(draws), shape[axis_at] // blocks).reshape((-1,) + (1,) * (len(shape) - 1 - axis_at))
    return level


def deal_out(own_key, own, number, rows, number_of, top, most, skew):
    ranking = jax.random.permutation(own_key, number_of)
    packed, ordinary = shares(number_of, rows * top, most, skew, True), shares(number_of, rows * top, most, skew, False)
    places = jnp.arange(number_of)

    def named(sizes, turn):
        used = int((sizes > 0).sum())
        fixed = max(1, used // 4)
        moved = fixed + (places - fixed + turn * (used - fixed)) % max(1, number_of - fixed)
        return jnp.zeros((number_of,), jnp.int32).at[ranking[jnp.where(places < fixed, places, moved)]].set(jnp.asarray(sizes, jnp.int32))

    sizes = jnp.where(number % 4 == 0, named(packed, number // 4), named(ordinary, number - number // 4 - 1))
    mixed = jax.random.permutation(jax.random.fold_in(own, 3), number_of)
    giver, taker = mixed[0:number_of // 2 * 2:2], mixed[1:number_of // 2 * 2:2]
    slack = jnp.minimum(sizes[giver] - 1, most - sizes[taker]) // 2
    slack = jnp.where((giver == ranking[0]) | (taker == ranking[0]) | (sizes[taker] == 0), 0, jnp.maximum(slack, 0))
    moved = jax.random.randint(jax.random.fold_in(own, 4), (number_of // 2,), 0, 1 << 20) % (slack + 1)
    sizes = sizes.at[giver].add(-moved).at[taker].add(moved)
    members = jnp.searchsorted(jnp.cumsum(sizes), jnp.arange(rows * top), side="right").astype(jnp.int32)
    listing = members.reshape(top, rows).T
    listing = listing[jax.random.permutation(jax.random.fold_in(own, 1), rows)]
    turn = jax.random.randint(jax.random.fold_in(own, 2), (rows, 1), 0, top)
    return jnp.take_along_axis(listing, (jnp.arange(top)[None, :] + turn) % top, axis=1)


def shares(amount, total, bound, slope, full):
    portions = [(1 << 20) // math.isqrt(rank ** slope) + 1 for rank in range(1, amount + 1)]
    largest = bound if full else min(bound, max(-(-total // amount), total * portions[0] // sum(portions)))
    least = 1 if total - largest >= amount - 1 else 0
    holding, rest = [largest] + [least] * (amount - 1), total - largest - least * (amount - 1)
    while rest > 0:
        movable = [i for i in range(1, amount) if holding[i] < largest] or [i for i in range(1, amount) if holding[i] < bound]
        mass, remaining = sum([portions[i] for i in movable]), rest
        for i in movable:
            addition = min(bound - holding[i], max(1, remaining * portions[i] // mass), rest)
            holding[i] = holding[i] + addition
            rest = rest - addition
    return np.array(holding)


def gaussian(rng, dims, scale, limit, shards=(), dtype=jnp.bfloat16):
    level = steps_of(rng, dims, shards, -0.22, 0.18) if shards else 1.0
    drawn = jax.random.normal(rng, dims, jnp.float32) * scale * level
    return jnp.minimum(jnp.maximum(drawn, -limit), limit).astype(dtype)


def setup_inputs(seed: int = 0) -> dict:
    arg_keys = jax.random.split(jax.random.key(seed), 7)
    hidden = gaussian(arg_keys[0], (REQUEST_COUNT, MODEL_WIDTH), 1.0, 6.0, ((0, 32),))
    key_value_weight = gaussian(arg_keys[1], (MODEL_WIDTH, 2 * KEY_VALUE_WIDTH), MODEL_WIDTH ** -0.5, 0.0625, ((1, 8),))
    request_group_keys = jax.random.split(jax.random.fold_in(arg_keys[2], 1), REQUEST_COUNT // ROWS_DEV)
    request_group_turns = jax.random.permutation(jax.random.fold_in(arg_keys[2], 3), REQUEST_COUNT // ROWS_DEV)
    request_group = jax.vmap(lambda own, number: deal_out(jax.random.fold_in(arg_keys[2], 2), own, number, ROWS_DEV, N_AD, 1, CAP, 2))(request_group_keys, request_group_turns).reshape((REQUEST_COUNT, 1))
    request_member = plant(jax.random.randint(arg_keys[3], (REQUEST_COUNT,), 0, ADP_DEV), jax.random.fold_in(arg_keys[3], 1), 0, ADP_DEV - 1).astype(jnp.int32)
    adapter_down_weight = gaussian(arg_keys[4], (MODEL_WIDTH, ADAPTER_COUNT * ADAPTER_RANK), MODEL_WIDTH ** -0.5, 0.0625, ((0, 8), (1, 32)))
    adapter_up_weight = gaussian(arg_keys[5], (ADAPTER_COUNT * ADAPTER_RANK, 2 * KEY_VALUE_WIDTH), ADAPTER_RANK ** -0.5, 0.75, ((0, 32), (1, 8)))
    return dict(hidden=hidden, key_value_weight=key_value_weight, request_group=request_group, request_member=request_member, adapter_down_weight=adapter_down_weight, adapter_up_weight=adapter_up_weight)


def reference(hidden, key_value_weight, request_group, request_member, adapter_down_weight, adapter_up_weight):
    base_output = jnp.dot(hidden, key_value_weight, preferred_element_type=jnp.float32)
    adapter_index = (request_group[:, 0] * ADP_DEV + request_member).astype(jnp.int32)
    down_matrix = adapter_down_weight.reshape(MODEL_WIDTH, ADAPTER_COUNT, ADAPTER_RANK)
    up_matrix = adapter_up_weight.reshape(ADAPTER_COUNT, ADAPTER_RANK, 2 * KEY_VALUE_WIDTH)
    block_total = REQUEST_COUNT // 16
    row_groupings = hidden.reshape(block_total, 16, MODEL_WIDTH)
    block_indices = adapter_index.reshape(block_total, 16)

    def block_quota(inputs):
        rows_block, ids_block = inputs
        down_rows = jnp.take(down_matrix, ids_block, axis=1)
        rank_values = jnp.einsum('rd,drk->rk', rows_block.astype(jnp.float32), down_rows.astype(jnp.float32)).astype(jnp.bfloat16)
        up_rows = jnp.take(up_matrix, ids_block, axis=0)
        return jnp.einsum('rk,rkv->rv', rank_values.astype(jnp.float32), up_rows.astype(jnp.float32)).astype(jnp.bfloat16)

    adapter_update = lax.map(block_quota, (row_groupings, block_indices)).reshape(REQUEST_COUNT, 2 * KEY_VALUE_WIDTH)
    return (base_output + adapter_update.astype(jnp.float32)).astype(jnp.bfloat16)
```

```python
import functools

import jax
import jax.numpy as jnp
from jax import lax
from jax.experimental import pallas as pl
from jax.experimental.pallas import tpu as pltpu
from jax.sharding import PartitionSpec as P

RANK = 64
SLOTS = 16
F32 = jnp.float32
BF16 = jnp.bfloat16
MESH = pl.DeviceIdType.MESH


def iota(shape, axis):
    return lax.broadcasted_iota(jnp.int32, shape, axis)


def kernel(
    nx, nz, ntp, hidden, weight, group, member, down, up, out,
    hcols, hbuf, wbuf, dbuf, ubuf, send, recv, meta_out, meta_in,
    part, parts, yout, yin,
    load_sem, base_sem, data_send, data_recv, meta_send, meta_recv,
    part_send, part_recv, ret_send, ret_recv,
):
    rows, depth = hidden.shape
    own = hcols.shape[1]
    wide = nz * SLOTS
    half = wide // 2
    members = dbuf.shape[1] // RANK
    ad = lax.axis_index("ad")
    tp = lax.axis_index("tp")
    x, z = ad // nz, lax.rem(ad, nz)

    def at(dx, dz):
        return {"ad": lax.rem(x + dx + nx, nx) * nz + lax.rem(z + dz + nz, nz)}

    def peer(o):
        return {"tp": lax.rem(tp + o, ntp)}

    offsets = [(dx, dz) for dx in range(nx) for dz in range(nz) if dx or dz]
    barrier = pltpu.get_barrier_semaphore()
    for dx, dz in offsets:
        pl.semaphore_signal(barrier, inc=1, device_id=at(dx, dz), device_id_type=MESH)
    for o in range(1, ntp):
        pl.semaphore_signal(barrier, inc=1, device_id=peer(o), device_id_type=MESH)

    first = pl.multiple_of(tp * own, own)
    loads = [
        pltpu.make_async_copy(hidden.at[:, pl.ds(first, own)], hcols, load_sem.at[0]),
        pltpu.make_async_copy(down, dbuf, load_sem.at[1]),
        pltpu.make_async_copy(up, ubuf, load_sem.at[2]),
    ]
    for load in loads:
        load.start()
    nk = depth // own
    base_loads = []
    for k in range(nk):
        cut = pl.ds(k * own, own)
        base_loads.append((
            pltpu.make_async_copy(hidden.at[:, cut], hbuf.at[k], base_sem.at[0, k]),
            pltpu.make_async_copy(weight.at[cut], wbuf.at[k], base_sem.at[1, k]),
        ))
    for pair in base_loads:
        for load in pair:
            load.start()

    goes = group[...]
    gx, gz = goes // nz, goes % nz
    rel = ((gx - x + nx) % nx) * nz + (gz - z + nz) % nz
    rel_across = rel.astype(F32)
    square = (rows, rows)
    down_at, across_at = iota(square, 0), iota(square, 1)
    rel_down = jnp.sum(jnp.where(down_at == across_at, rel_across, 0.0), axis=1, keepdims=True)
    same = (rel_down == rel_across).astype(F32)
    k_across = jnp.sum(jnp.where(down_at < across_at, same, 0.0), axis=0, keepdims=True)
    k_down = jnp.sum(jnp.where(across_at < down_at, same, 0.0), axis=1, keepdims=True)
    slot_across = (rel_across * SLOTS + k_across).astype(jnp.int32)
    slot_down = (rel_down * SLOTS + k_down).astype(jnp.int32)
    nd = nx * nz
    named = jnp.where(
        iota((nd, rows), 0) == rel_across.astype(jnp.int32), member[...].astype(F32), 0.0
    ).astype(BF16)
    placed = (iota((rows, 128), 1) == k_down.astype(jnp.int32)).astype(F32).astype(BF16)
    meta = jnp.dot(named, placed, preferred_element_type=F32)
    meta_out[...] = meta.reshape(nd, 1, 128)
    meta_in[0] = meta_out[0]

    loads[0].wait()
    mine = hcols[...]
    for c in range(nx):
        pick = (iota((wide, rows), 0) + c * wide == slot_across).astype(F32).astype(BF16)
        send[c] = jnp.dot(pick, mine, preferred_element_type=F32).astype(BF16)
    recv[0, :SLOTS] = send[0, :SLOTS]

    pl.semaphore_wait(barrier, len(offsets) + ntp - 1)

    metas = []
    for dx, dz in offsets:
        i = dx * nz + dz
        metas.append(pltpu.make_async_remote_copy(
            meta_out.at[i], meta_in.at[i], meta_send, meta_recv,
            device_id=at(dx, dz), device_id_type=MESH))
        metas[-1].start()
    order = sorted(range(nz), key=lambda dz: -min(dz, nz - dz))
    for dx in range(nx):
        for dz in order:
            if dx or dz:
                cut = pl.ds(dz * SLOTS, SLOTS)
                pltpu.make_async_remote_copy(
                    send.at[dx, cut], recv.at[dx, cut], data_send.at[dx], data_recv.at[dx],
                    device_id=at(dx, dz), device_id_type=MESH).start()

    base = jnp.zeros((rows, out.shape[1]), F32)
    for k in range(nk):
        for load in base_loads[k]:
            load.wait()
        base = base + jnp.dot(hbuf[k], wbuf[k], preferred_element_type=F32)

    loads[1].wait()
    loads[2].wait()

    def whole(ref, sem):
        return pltpu.make_async_copy(ref, ref, sem)

    whole(meta_in.at[pl.ds(1, nd - 1)], meta_recv).wait()
    left = iota((half, 128), 1) < RANK
    block = iota((wide, members * RANK), 1) // RANK

    def kept(c):
        m = meta_in[c * nz:(c + 1) * nz]
        m = jnp.broadcast_to(m, (nz, SLOTS, 128)).reshape(wide, 128)
        hit = iota((wide, 128), 1) == iota((wide, 128), 0) % SLOTS
        m = jnp.sum(jnp.where(hit, m, 0.0), axis=1, keepdims=True)
        return block == m.astype(jnp.int32)

    def project(c):
        if c == 0:
            whole(recv.at[0, pl.ds(SLOTS, wide - SLOTS)], data_recv.at[0]).wait()
        else:
            whole(recv.at[c], data_recv.at[c]).wait()
        scores = jnp.dot(recv[c], dbuf[...], preferred_element_type=F32)
        scores = jnp.where(kept(c), scores, 0.0)
        total = scores[:, :128]
        for j in range(1, members * RANK // 128):
            total = total + scores[:, j * 128:(j + 1) * 128]
        total = total + pltpu.roll(total, RANK, 1)
        packed = jnp.where(left, total[:half], total[half:])
        part[c] = packed.astype(BF16)
        for o in range(1, ntp):
            pltpu.make_async_remote_copy(
                part.at[c], parts.at[c, o - 1], part_send.at[c], part_recv.at[c],
                device_id=peer(o), device_id_type=MESH).start()
        return packed

    def raise_up(c, packed):
        whole(parts.at[c], part_recv.at[c]).wait()
        total = packed
        for o in range(1, ntp):
            total = total + parts[c, o - 1].astype(F32)
        turned = pltpu.roll(total, RANK, 1)
        both = jnp.concatenate(
            [jnp.where(left, total, turned), jnp.where(left, turned, total)], axis=0)
        spread = jnp.concatenate([both] * (members * RANK // 128), axis=1)
        spread = jnp.where(kept(c), spread, 0.0).astype(BF16)
        yout[c] = jnp.dot(spread, ubuf[...], preferred_element_type=F32).astype(BF16)
        for dz in order:
            if c or dz:
                cut = pl.ds(dz * SLOTS, SLOTS)
                pltpu.make_async_remote_copy(
                    yout.at[c, cut], yin.at[c, cut], ret_send.at[c], ret_recv.at[c],
                    device_id=at(-c, -dz), device_id_type=MESH).start()
            else:
                yin[0, :SLOTS] = yout[0, :SLOTS]

    packed = project(0)
    for c in range(1, nx):
        following = project(c)
        raise_up(c - 1, packed)
        packed = following
    raise_up(nx - 1, packed)

    delta = jnp.zeros((rows, out.shape[1]), F32)
    for c in range(nx):
        cut = yin.at[0, pl.ds(SLOTS, wide - SLOTS)] if c == 0 else yin.at[c]
        whole(cut, ret_recv.at[c]).wait()
        pick = (iota((rows, wide), 1) + c * wide == slot_down).astype(F32).astype(BF16)
        delta = delta + jnp.dot(pick, yin[c], preferred_element_type=F32)
    out[...] = (base + delta).astype(BF16)

    whole(meta_out.at[pl.ds(1, nd - 1)], meta_send).wait()
    for c in range(nx):
        tail = pl.ds(SLOTS, wide - SLOTS)
        whole(send.at[0, tail] if c == 0 else send.at[c], data_send.at[c]).wait()
        whole(yout.at[0, tail] if c == 0 else yout.at[c], ret_send.at[c]).wait()
        whole(parts.at[c], part_send.at[c]).wait()


def build(mesh, nx, nz):
    ntp = mesh.shape["tp"]

    def step(hidden, weight, group, member, down, up):
        rows, depth = hidden.shape
        own, ranks = down.shape
        features = weight.shape[1]
        wide = nz * SLOTS
        nk = depth // own
        nd = nx * nz
        vmem = pl.BlockSpec(memory_space=pltpu.VMEM)
        hbm = pl.BlockSpec(memory_space=pl.ANY)
        dma = pltpu.SemaphoreType.DMA
        return pl.pallas_call(
            functools.partial(kernel, nx, nz, ntp),
            out_shape=jax.ShapeDtypeStruct((rows, features), BF16),
            in_specs=[hbm, hbm, vmem, vmem, hbm, hbm],
            out_specs=vmem,
            scratch_shapes=[
                pltpu.VMEM((rows, own), BF16),
                pltpu.VMEM((nk, rows, own), BF16),
                pltpu.VMEM((nk, own, features), BF16),
                pltpu.VMEM((own, ranks), BF16),
                pltpu.VMEM((ranks, features), BF16),
                pltpu.VMEM((nx, wide, own), BF16),
                pltpu.VMEM((nx, wide, own), BF16),
                pltpu.VMEM((nd, 1, 128), F32),
                pltpu.VMEM((nd, 1, 128), F32),
                pltpu.VMEM((nx, wide // 2, 128), BF16),
                pltpu.VMEM((nx, ntp - 1, wide // 2, 128), BF16),
                pltpu.VMEM((nx, wide, features), BF16),
                pltpu.VMEM((nx, wide, features), BF16),
                dma((3,)), dma((2, nk)), dma((nx,)), dma((nx,)), dma, dma,
                dma((nx,)), dma((nx,)), dma((nx,)), dma((nx,)),
            ],
            compiler_params=pltpu.CompilerParams(
                collective_id=0, has_side_effects=True, vmem_limit_bytes=56 * 1024 * 1024
            ),
        )(hidden, weight, group.reshape(1, rows), member.reshape(1, rows), down, up)

    placed = (P("ad", None), P(None, "tp"), P("ad", None), P("ad"), P("tp", "ad"), P("ad", "tp"))
    return jax.shard_map(
        step, mesh=mesh, in_specs=placed, out_specs=P("ad", "tp"), check_vma=False
    )


def solution(mesh):
    return build(mesh, 4, 8)
```

```python
import functools

import jax
import jax.numpy as jnp
from jax import lax
from jax.experimental import pallas as pl
from jax.experimental.pallas import tpu as pltpu
from jax.sharding import PartitionSpec as P

RANK = 64
SLOTS = 16
F32 = jnp.float32
BF16 = jnp.bfloat16
CHUNKS = ((0, 12), (12, 20), (20, 28), (28, 32))
MESH = pl.DeviceIdType.MESH


def iota(shape, axis):
    return lax.broadcasted_iota(jnp.int32, shape, axis)


def kernel(
    nx, nz, ntp, chunks, hidden, weight, group, member, down, up, out,
    hcols, hbuf, wbuf, dbuf, ubuf, send, recv, meta_out, meta_in,
    part, parts, yout, yin,
    load_sem, base_sem, data_send, data_recv, meta_send, meta_recv,
    part_send, part_recv, ret_send, ret_recv,
):
    rows, depth = hidden.shape
    own = hcols.shape[1]
    members = dbuf.shape[1] // RANK
    ad = lax.axis_index("ad")
    tp = lax.axis_index("tp")
    x, z = ad // nz, lax.rem(ad, nz)

    def at(dx, dz):
        return {"ad": lax.rem(x + dx + nx, nx) * nz + lax.rem(z + dz + nz, nz)}

    def peer(o):
        return {"tp": lax.rem(tp + o, ntp)}

    by_z = [nz // 2] + [d for k in range(nz // 2 - 1, 0, -1) for d in (k, nz - k)] + [0]
    by_x = [nx // 2] + [d for k in range(nx // 2 - 1, 0, -1) for d in (k, nx - k)] + [0]
    spots = [(dx, dz) for dz in by_z for dx in by_x]
    offsets = spots[:-1]
    first = pl.multiple_of(tp * own, own)
    own_load = pltpu.make_async_copy(hidden.at[:, pl.ds(first, own)], hcols, load_sem.at[0])
    own_load.start()

    barrier = pltpu.get_barrier_semaphore()
    for dx, dz in offsets:
        pl.semaphore_signal(barrier, inc=1, device_id=at(dx, dz), device_id_type=MESH)
    for o in range(1, ntp):
        pl.semaphore_signal(barrier, inc=1, device_id=peer(o), device_id_type=MESH)

    goes = group[...]
    gx, gz = goes // nz, goes % nz

    def place(d, n):
        return jnp.where(d > n // 2, (d - n // 2) * 2, jnp.maximum((n // 2 - d) * 2 - 1, 0))

    rel = place((gz - z + nz) % nz, nz) * nx + place((gx - x + nx) % nx, nx)
    rel_across = rel.astype(F32)
    square = (rows, rows)
    down_at, across_at = iota(square, 0), iota(square, 1)
    rel_down = jnp.sum(jnp.where(down_at == across_at, rel_across, 0.0), axis=1, keepdims=True)
    same = (rel_down == rel_across).astype(F32)
    k_across = jnp.sum(jnp.where(down_at < across_at, same, 0.0), axis=0, keepdims=True)
    k_down = jnp.sum(jnp.where(across_at < down_at, same, 0.0), axis=1, keepdims=True)
    slot_across = (rel_across * SLOTS + k_across).astype(jnp.int32)
    slot_down = (rel_down * SLOTS + k_down).astype(jnp.int32)
    nd = nx * nz
    named = jnp.where(
        iota((nd, rows), 0) == rel_across.astype(jnp.int32), member[...].astype(F32), 0.0
    ).astype(BF16)
    placed = (iota((rows, 128), 1) == k_down.astype(jnp.int32)).astype(F32).astype(BF16)
    meta = jnp.dot(named, placed, preferred_element_type=F32)
    meta_out[...] = meta.reshape(nd, 1, 128)
    meta_in[nd - 1] = meta_out[nd - 1]

    own_load.wait()
    mine = hcols[...]
    self_at = (nd - 1) * SLOTS

    def gather(c):
        lo, hi = chunks[c]
        n = (hi - lo) * SLOTS
        pick = (iota((n, rows), 0) + lo * SLOTS == slot_across).astype(F32).astype(BF16)
        send[lo * SLOTS:hi * SLOTS] = jnp.dot(pick, mine, preferred_element_type=F32).astype(BF16)

    def issue(c):
        for i in range(*chunks[c]):
            if i < nd - 1:
                cut = pl.ds(i * SLOTS, SLOTS)
                pltpu.make_async_remote_copy(
                    send.at[cut], recv.at[cut], data_send.at[c], data_recv.at[c],
                    device_id=at(*spots[i]), device_id_type=MESH).start()

    gather(0)
    pl.semaphore_wait(barrier, len(offsets) + ntp - 1)
    issue(0)
    for i, (dx, dz) in enumerate(offsets):
        pltpu.make_async_remote_copy(
            meta_out.at[i], meta_in.at[i], meta_send, meta_recv,
            device_id=at(dx, dz), device_id_type=MESH).start()
    for c in range(1, len(chunks)):
        gather(c)
        issue(c)
    recv[self_at:] = send[self_at:]

    loads = [
        pltpu.make_async_copy(down, dbuf, load_sem.at[1]),
        pltpu.make_async_copy(up, ubuf, load_sem.at[2]),
    ]
    for load in loads:
        load.start()
    nk = depth // own
    base_loads = []
    for k in range(nk):
        cut = pl.ds(k * own, own)
        base_loads.append((
            pltpu.make_async_copy(hidden.at[:, cut], hbuf.at[k], base_sem.at[0, k]),
            pltpu.make_async_copy(weight.at[cut], wbuf.at[k], base_sem.at[1, k]),
        ))
    for pair in base_loads:
        for load in pair:
            load.start()

    base = jnp.zeros((rows, out.shape[1]), F32)
    for k in range(nk):
        for load in base_loads[k]:
            load.wait()
        base = base + jnp.dot(hbuf[k], wbuf[k], preferred_element_type=F32)

    for load in loads:
        load.wait()

    def whole(ref, sem):
        return pltpu.make_async_copy(ref, ref, sem)

    def away(ref, c):
        lo, hi = chunks[c]
        return ref.at[pl.ds(lo * SLOTS, (min(hi, nd - 1) - lo) * SLOTS)]

    whole(meta_in.at[pl.ds(0, nd - 1)], meta_recv).wait()

    def kept(c):
        lo, hi = chunks[c]
        n = (hi - lo) * SLOTS
        m = jnp.broadcast_to(meta_in[lo:hi], (hi - lo, SLOTS, 128)).reshape(n, 128)
        hit = iota((n, 128), 1) == iota((n, 128), 0) % SLOTS
        m = jnp.sum(jnp.where(hit, m, 0.0), axis=1, keepdims=True)
        return iota((n, members * RANK), 1) // RANK == m.astype(jnp.int32)

    def halves(c):
        lo, hi = chunks[c]
        half = (hi - lo) * SLOTS // 2
        return half, lo * SLOTS // 2

    def project(c):
        lo, hi = chunks[c]
        half, first = halves(c)
        keep = kept(c)
        whole(away(recv, c), data_recv.at[c]).wait()
        scores = jnp.dot(recv[lo * SLOTS:hi * SLOTS], dbuf[...], preferred_element_type=F32)
        scores = jnp.where(keep, scores, 0.0)
        total = scores[:, :128]
        for j in range(1, members * RANK // 128):
            total = total + scores[:, j * 128:(j + 1) * 128]
        total = total + pltpu.roll(total, RANK, 1)
        packed = jnp.where(iota((half, 128), 1) < RANK, total[:half], total[half:])
        part[first:first + half] = packed.astype(BF16)
        for o in range(1, ntp):
            pltpu.make_async_remote_copy(
                part.at[pl.ds(first, half)],
                parts.at[pl.ds(first * (ntp - 1) + (o - 1) * half, half)],
                part_send.at[c], part_recv.at[c],
                device_id=peer(o), device_id_type=MESH).start()
        return packed, keep

    def landed(c):
        half, first = halves(c)
        return parts.at[pl.ds(first * (ntp - 1), half * (ntp - 1))]

    def raise_up(c, packed, keep):
        lo, hi = chunks[c]
        half, first = halves(c)
        whole(landed(c), part_recv.at[c]).wait()
        total = packed
        for o in range(ntp - 1):
            start = first * (ntp - 1) + o * half
            total = total + parts[start:start + half].astype(F32)
        turned = pltpu.roll(total, RANK, 1)
        left = iota((half, 128), 1) < RANK
        both = jnp.concatenate(
            [jnp.where(left, total, turned), jnp.where(left, turned, total)], axis=0)
        spread = jnp.concatenate([both] * (members * RANK // 128), axis=1)
        spread = jnp.where(keep, spread, 0.0).astype(BF16)
        yout[lo * SLOTS:hi * SLOTS] = jnp.dot(
            spread, ubuf[...], preferred_element_type=F32).astype(BF16)
        for i in range(lo, hi):
            cut = pl.ds(i * SLOTS, SLOTS)
            if i < nd - 1:
                dx, dz = spots[i]
                pltpu.make_async_remote_copy(
                    yout.at[cut], yin.at[cut], ret_send.at[c], ret_recv.at[c],
                    device_id=at(-dx, -dz), device_id_type=MESH).start()
            else:
                yin[self_at:] = yout[self_at:]

    held = [project(c) for c in range(len(chunks))]
    for c, kept_ranks in enumerate(held):
        raise_up(c, *kept_ranks)

    delta = base
    for c, (lo, hi) in enumerate(chunks):
        n = (hi - lo) * SLOTS
        pick = (iota((rows, n), 1) + lo * SLOTS == slot_down).astype(F32).astype(BF16)
        whole(away(yin, c), ret_recv.at[c]).wait()
        delta = delta + jnp.dot(pick, yin[lo * SLOTS:hi * SLOTS], preferred_element_type=F32)
    out[...] = delta.astype(BF16)

    whole(meta_out.at[pl.ds(0, nd - 1)], meta_send).wait()
    for c in range(len(chunks)):
        whole(away(send, c), data_send.at[c]).wait()
        whole(away(yout, c), ret_send.at[c]).wait()
        whole(landed(c), part_send.at[c]).wait()


def build(mesh, nx, nz, chunks):
    ntp = mesh.shape["tp"]

    def step(hidden, weight, group, member, down, up):
        rows, depth = hidden.shape
        own, ranks = down.shape
        features = weight.shape[1]
        nk = depth // own
        nd = nx * nz
        total = nd * SLOTS
        nc = len(chunks)
        vmem = pl.BlockSpec(memory_space=pltpu.VMEM)
        hbm = pl.BlockSpec(memory_space=pl.ANY)
        dma = pltpu.SemaphoreType.DMA
        return pl.pallas_call(
            functools.partial(kernel, nx, nz, ntp, chunks),
            out_shape=jax.ShapeDtypeStruct((rows, features), BF16),
            in_specs=[hbm, hbm, vmem, vmem, hbm, hbm],
            out_specs=vmem,
            scratch_shapes=[
                pltpu.VMEM((rows, own), BF16),
                pltpu.VMEM((nk, rows, own), BF16),
                pltpu.VMEM((nk, own, features), BF16),
                pltpu.VMEM((own, ranks), BF16),
                pltpu.VMEM((ranks, features), BF16),
                pltpu.VMEM((total, own), BF16),
                pltpu.VMEM((total, own), BF16),
                pltpu.VMEM((nd, 1, 128), F32),
                pltpu.VMEM((nd, 1, 128), F32),
                pltpu.VMEM((total // 2, 128), BF16),
                pltpu.VMEM(((ntp - 1) * total // 2, 128), BF16),
                pltpu.VMEM((total, features), BF16),
                pltpu.VMEM((total, features), BF16),
                dma((3,)), dma((2, nk)), dma((nc,)), dma((nc,)), dma, dma,
                dma((nc,)), dma((nc,)), dma((nc,)), dma((nc,)),
            ],
            compiler_params=pltpu.CompilerParams(
                collective_id=0, has_side_effects=True, vmem_limit_bytes=56 * 1024 * 1024
            ),
        )(hidden, weight, group.reshape(1, rows), member.reshape(1, rows), down, up)

    placed = (P("ad", None), P(None, "tp"), P("ad", None), P("ad"), P("tp", "ad"), P("ad", "tp"))
    return jax.shard_map(
        step, mesh=mesh, in_specs=placed, out_specs=P("ad", "tp"), check_vma=False
    )


def solution(mesh):
    return build(mesh, 4, 8, CHUNKS)
```

```python
import functools

import jax
import jax.numpy as jnp
from jax import lax
from jax.experimental import pallas as pl
from jax.experimental.pallas import tpu as pltpu
from jax.sharding import PartitionSpec as P

RANK = 64
SLOTS = 16
F32 = jnp.float32
BF16 = jnp.bfloat16
MESH = pl.DeviceIdType.MESH


def iota(shape, axis):
    return lax.broadcasted_iota(jnp.int32, shape, axis)


def kernel(
    nx, nz, ntp, plan, hidden, weight, group, member, down, up, out,
    hcols, hbuf, wbuf, dbuf, ubuf, send, recv, meta_out, meta_in,
    part, parts, yout, yin,
    load_sem, base_sem, data_send, data_recv, meta_send, meta_recv,
    part_send, part_recv, ret_send, ret_recv, ready,
):
    rows, depth = hidden.shape
    own = hcols.shape[1]
    members = dbuf.shape[1] // RANK
    ad = lax.axis_index("ad")
    tp = lax.axis_index("tp")
    x, z = ad // nz, lax.rem(ad, nz)

    def at(dx, dz):
        return {"ad": lax.rem(x + dx + nx, nx) * nz + lax.rem(z + dz + nz, nz)}

    def peer(o):
        return {"tp": lax.rem(tp + o, ntp)}

    spots = [spot for chunk in plan for spot in chunk]
    chunks, nd = [], 0
    for chunk in plan:
        chunks.append((nd, nd + len(chunk)))
        nd += len(chunk)
    offsets = spots[:-1]
    first = pl.multiple_of(tp * own, own)
    own_load = pltpu.make_async_copy(hidden.at[:, pl.ds(first, own)], hcols, load_sem.at[0])
    own_load.start()

    barrier = pltpu.get_barrier_semaphore()
    greeted = [(0, dz) for dz in range(1, nz)] + [(dx, 0) for dx in range(1, nx)]
    for dx, dz in greeted:
        pl.semaphore_signal(barrier, inc=1, device_id=at(dx, dz), device_id_type=MESH)
    for o in range(1, ntp):
        pl.semaphore_signal(barrier, inc=1, device_id=peer(o), device_id_type=MESH)

    goes = group[...]
    gx, gz = goes // nz, goes % nz

    code = (gx - x + nx) % nx * nz + (gz - z + nz) % nz
    rel = jnp.zeros_like(code)
    for i, (dx, dz) in enumerate(spots):
        rel = jnp.where(code == dx * nz + dz, i, rel)
    rel_across = rel.astype(F32)
    square = (rows, rows)
    down_at, across_at = iota(square, 0), iota(square, 1)
    rel_down = jnp.sum(jnp.where(down_at == across_at, rel_across, 0.0), axis=1, keepdims=True)
    same = (rel_down == rel_across).astype(F32)
    k_across = jnp.sum(jnp.where(down_at < across_at, same, 0.0), axis=0, keepdims=True)
    k_down = jnp.sum(jnp.where(across_at < down_at, same, 0.0), axis=1, keepdims=True)
    slot_across = (rel_across * SLOTS + k_across).astype(jnp.int32)
    slot_down = (rel_down * SLOTS + k_down).astype(jnp.int32)
    named = jnp.where(
        iota((nd, rows), 0) == rel_across.astype(jnp.int32), member[...].astype(F32), 0.0
    ).astype(BF16)
    placed = (iota((rows, 128), 1) == k_down.astype(jnp.int32)).astype(F32).astype(BF16)
    meta = jnp.dot(named, placed, preferred_element_type=F32)
    meta_out[...] = meta.reshape(nd, 1, 128)
    meta_in[nd - 1] = meta_out[nd - 1]

    own_load.wait()
    mine = hcols[...]
    self_at = (nd - 1) * SLOTS

    def gather(c):
        lo, hi = chunks[c]
        n = (hi - lo) * SLOTS
        pick = (iota((n, rows), 0) + lo * SLOTS == slot_across).astype(F32).astype(BF16)
        send[lo * SLOTS:hi * SLOTS] = jnp.dot(pick, mine, preferred_element_type=F32).astype(BF16)

    def issue(c):
        for i in range(*chunks[c]):
            if i < nd - 1:
                cut = pl.ds(i * SLOTS, SLOTS)
                pltpu.make_async_remote_copy(
                    send.at[cut], recv.at[cut], data_send.at[c], data_recv.at[c],
                    device_id=at(*spots[i]), device_id_type=MESH).start()

    def tell(c):
        lo, hi = chunks[c]
        for i in range(lo, min(hi, nd - 1)):
            pltpu.make_async_remote_copy(
                meta_out.at[i], meta_in.at[i], meta_send.at[c], meta_recv.at[c],
                device_id=at(*spots[i]), device_id_type=MESH).start()

    gather(0)
    pl.semaphore_wait(barrier, len(greeted) + ntp - 1)
    for dx in range(1, nx):
        pl.semaphore_signal(
            ready.at[nx - dx - 1], inc=1, device_id=at(dx, 0), device_id_type=MESH)
    tell(0)
    issue(0)
    unheard = set(range(1, nx))
    for c in range(1, len(chunks)):
        gather(c)
        for dx in sorted({dx for dx, dz in plan[c] if dz} & unheard):
            pl.semaphore_wait(ready.at[dx - 1], 1)
            unheard.remove(dx)
        tell(c)
        issue(c)
    recv[self_at:] = send[self_at:]

    loads = [
        pltpu.make_async_copy(down, dbuf, load_sem.at[1]),
        pltpu.make_async_copy(up, ubuf, load_sem.at[2]),
    ]
    for load in loads:
        load.start()
    nk = depth // own
    base_loads = []
    for k in range(nk):
        cut = pl.ds(k * own, own)
        base_loads.append((
            pltpu.make_async_copy(hidden.at[:, cut], hbuf.at[k], base_sem.at[0, k]),
            pltpu.make_async_copy(weight.at[cut], wbuf.at[k], base_sem.at[1, k]),
        ))
    for pair in base_loads:
        for load in pair:
            load.start()

    base = jnp.zeros((rows, out.shape[1]), F32)
    for k in range(nk):
        for load in base_loads[k]:
            load.wait()
        base = base + jnp.dot(hbuf[k], wbuf[k], preferred_element_type=F32)

    for load in loads:
        load.wait()

    def whole(ref, sem):
        return pltpu.make_async_copy(ref, ref, sem)

    def away(ref, c):
        lo, hi = chunks[c]
        return ref.at[pl.ds(lo * SLOTS, (min(hi, nd - 1) - lo) * SLOTS)]

    def told(ref, c):
        lo, hi = chunks[c]
        return ref.at[pl.ds(lo, min(hi, nd - 1) - lo)]

    def kept(c):
        lo, hi = chunks[c]
        n = (hi - lo) * SLOTS
        m = jnp.broadcast_to(meta_in[lo:hi], (hi - lo, SLOTS, 128)).reshape(n, 128)
        hit = iota((n, 128), 1) == iota((n, 128), 0) % SLOTS
        m = jnp.sum(jnp.where(hit, m, 0.0), axis=1, keepdims=True)
        return iota((n, members * RANK), 1) // RANK == m.astype(jnp.int32)

    def halves(c):
        lo, hi = chunks[c]
        half = (hi - lo) * SLOTS // 2
        return half, lo * SLOTS // 2

    def project(c):
        lo, hi = chunks[c]
        half, first = halves(c)
        whole(told(meta_in, c), meta_recv.at[c]).wait()
        keep = kept(c)
        whole(away(recv, c), data_recv.at[c]).wait()
        scores = jnp.dot(recv[lo * SLOTS:hi * SLOTS], dbuf[...], preferred_element_type=F32)
        scores = jnp.where(keep, scores, 0.0)
        total = scores[:, :128]
        for j in range(1, members * RANK // 128):
            total = total + scores[:, j * 128:(j + 1) * 128]
        total = total + pltpu.roll(total, RANK, 1)
        packed = jnp.where(iota((half, 128), 1) < RANK, total[:half], total[half:])
        part[first:first + half] = packed.astype(BF16)
        for o in range(1, ntp):
            pltpu.make_async_remote_copy(
                part.at[pl.ds(first, half)],
                parts.at[pl.ds(first * (ntp - 1) + (o - 1) * half, half)],
                part_send.at[c], part_recv.at[c],
                device_id=peer(o), device_id_type=MESH).start()
        return packed, keep

    def landed(c):
        half, first = halves(c)
        return parts.at[pl.ds(first * (ntp - 1), half * (ntp - 1))]

    def raise_up(c, packed, keep):
        lo, hi = chunks[c]
        half, first = halves(c)
        whole(landed(c), part_recv.at[c]).wait()
        total = packed
        for o in range(ntp - 1):
            start = first * (ntp - 1) + o * half
            total = total + parts[start:start + half].astype(F32)
        turned = pltpu.roll(total, RANK, 1)
        left = iota((half, 128), 1) < RANK
        both = jnp.concatenate(
            [jnp.where(left, total, turned), jnp.where(left, turned, total)], axis=0)
        spread = jnp.concatenate([both] * (members * RANK // 128), axis=1)
        spread = jnp.where(keep, spread, 0.0).astype(BF16)
        yout[lo * SLOTS:hi * SLOTS] = jnp.dot(
            spread, ubuf[...], preferred_element_type=F32).astype(BF16)
        for i in range(lo, hi):
            cut = pl.ds(i * SLOTS, SLOTS)
            if i < nd - 1:
                dx, dz = spots[i]
                pltpu.make_async_remote_copy(
                    yout.at[cut], yin.at[cut], ret_send.at[c], ret_recv.at[c],
                    device_id=at(-dx, -dz), device_id_type=MESH).start()
            else:
                yin[self_at:] = yout[self_at:]

    held = [project(c) for c in range(len(chunks))]
    for c, kept_ranks in enumerate(held):
        raise_up(c, *kept_ranks)

    delta = base
    for c, (lo, hi) in enumerate(chunks):
        n = (hi - lo) * SLOTS
        pick = (iota((rows, n), 1) + lo * SLOTS == slot_down).astype(F32).astype(BF16)
        whole(away(yin, c), ret_recv.at[c]).wait()
        delta = delta + jnp.dot(pick, yin[lo * SLOTS:hi * SLOTS], preferred_element_type=F32)
    out[...] = delta.astype(BF16)

    for c in range(len(chunks)):
        whole(told(meta_out, c), meta_send.at[c]).wait()
        whole(away(send, c), data_send.at[c]).wait()
        whole(away(yout, c), ret_send.at[c]).wait()
        whole(landed(c), part_send.at[c]).wait()


def build(mesh, nx, nz, plan):
    ntp = mesh.shape["tp"]

    def step(hidden, weight, group, member, down, up):
        rows, depth = hidden.shape
        own, ranks = down.shape
        features = weight.shape[1]
        nk = depth // own
        nd = nx * nz
        total = nd * SLOTS
        nc = len(plan)
        vmem = pl.BlockSpec(memory_space=pltpu.VMEM)
        hbm = pl.BlockSpec(memory_space=pl.ANY)
        dma = pltpu.SemaphoreType.DMA
        return pl.pallas_call(
            functools.partial(kernel, nx, nz, ntp, plan),
            out_shape=pltpu.VMEM((rows, features), BF16),
            in_specs=[hbm, hbm, vmem, vmem, hbm, hbm],
            out_specs=vmem,
            scratch_shapes=[
                pltpu.VMEM((rows, own), BF16),
                pltpu.VMEM((nk, rows, own), BF16),
                pltpu.VMEM((nk, own, features), BF16),
                pltpu.VMEM((own, ranks), BF16),
                pltpu.VMEM((ranks, features), BF16),
                pltpu.VMEM((total, own), BF16),
                pltpu.VMEM((total, own), BF16),
                pltpu.VMEM((nd, 1, 128), F32),
                pltpu.VMEM((nd, 1, 128), F32),
                pltpu.VMEM((total // 2, 128), BF16),
                pltpu.VMEM(((ntp - 1) * total // 2, 128), BF16),
                pltpu.VMEM((total, features), BF16),
                pltpu.VMEM((total, features), BF16),
                dma((3,)), dma((2, nk)), dma((nc,)), dma((nc,)), dma((nc,)), dma((nc,)),
                dma((nc,)), dma((nc,)), dma((nc,)), dma((nc,)),
                pltpu.SemaphoreType.REGULAR((nx - 1,)),
            ],
            compiler_params=pltpu.CompilerParams(
                collective_id=0, has_side_effects=True, vmem_limit_bytes=56 * 1024 * 1024
            ),
        )(hidden, weight, group.reshape(1, rows), member.reshape(1, rows), down, up)

    placed = (P("ad", None), P(None, "tp"), P("ad", None), P("ad"), P("tp", "ad"), P("ad", "tp"))
    return jax.shard_map(
        step, mesh=mesh, in_specs=placed, out_specs=P("ad", "tp"), check_vma=False
    )


def plan():
    far = (4, 3, 5, 2, 6, 1, 7)
    spots = [(0, dz) for dz in far[:3]] + [(2, 0), (1, 0), (3, 0)]
    spots += [(dx, dz) for dx in (2, 1, 3) for dz in far]
    spots += [(0, dz) for dz in far[3:]] + [(0, 0)]
    ends = (6, 14, 20, 26, 32)
    return [spots[lo:hi] for lo, hi in zip((0,) + ends, ends)]


def solution(mesh):
    return build(mesh, 4, 8, plan())
```

```python
import functools

import jax
import jax.numpy as jnp
from jax import lax
from jax.experimental import pallas as pl
from jax.experimental.pallas import tpu as pltpu
from jax.sharding import PartitionSpec as P

RANK = 64
SLOTS = 16
F32 = jnp.float32
BF16 = jnp.bfloat16
MESH = pl.DeviceIdType.MESH


def iota(shape, axis):
    return lax.broadcasted_iota(jnp.int32, shape, axis)


def kernel(
    nx, nz, ntp, plan, hidden, weight, group, member, down, up, out,
    hcols, hbuf, wbuf, dbuf, ubuf, send, recv, meta_out, meta_in,
    part, parts, yout, yin,
    load_sem, base_sem, data_send, data_recv, meta_send, meta_recv,
    part_send, part_recv, ret_send, ret_recv, ready,
):
    rows, depth = hidden.shape
    own = hcols.shape[1]
    members = dbuf.shape[1] // RANK
    ad = lax.axis_index("ad")
    tp = lax.axis_index("tp")
    x, z = ad // nz, lax.rem(ad, nz)

    def at(dx, dz):
        return {"ad": lax.rem(x + dx + nx, nx) * nz + lax.rem(z + dz + nz, nz)}

    def peer(o):
        return {"tp": lax.rem(tp + o, ntp)}

    spots = [spot for chunk in plan for spot in chunk]
    chunks, nd = [], 0
    for chunk in plan:
        chunks.append((nd, nd + len(chunk)))
        nd += len(chunk)
    offsets = spots[:-1]
    first = pl.multiple_of(tp * own, own)
    own_load = pltpu.make_async_copy(hidden.at[:, pl.ds(first, own)], hcols, load_sem.at[0])
    own_load.start()

    barrier = pltpu.get_barrier_semaphore()
    greeted = [(0, dz) for dz in range(1, nz)] + [(dx, 0) for dx in range(1, nx)]
    for dx, dz in greeted:
        pl.semaphore_signal(barrier, inc=1, device_id=at(dx, dz), device_id_type=MESH)
    for o in range(1, ntp):
        pl.semaphore_signal(barrier, inc=1, device_id=peer(o), device_id_type=MESH)

    goes = group[...]
    gx, gz = goes // nz, goes % nz

    code = (gx - x + nx) % nx * nz + (gz - z + nz) % nz
    rel = jnp.zeros_like(code)
    for i, (dx, dz) in enumerate(spots):
        rel = jnp.where(code == dx * nz + dz, i, rel)
    rel_across = rel.astype(F32)
    square = (rows, rows)
    down_at, across_at = iota(square, 0), iota(square, 1)
    rel_down = jnp.sum(jnp.where(down_at == across_at, rel_across, 0.0), axis=1, keepdims=True)
    same = (rel_down == rel_across).astype(F32)
    k_across = jnp.sum(jnp.where(down_at < across_at, same, 0.0), axis=0, keepdims=True)
    k_down = jnp.sum(jnp.where(across_at < down_at, same, 0.0), axis=1, keepdims=True)
    slot_across = (rel_across * SLOTS + k_across).astype(jnp.int32)
    slot_down = (rel_down * SLOTS + k_down).astype(jnp.int32)
    named = jnp.where(
        iota((nd, rows), 0) == rel_across.astype(jnp.int32), member[...].astype(F32), 0.0
    ).astype(BF16)
    placed = (iota((rows, 128), 1) == k_down.astype(jnp.int32)).astype(F32).astype(BF16)
    meta = jnp.dot(named, placed, preferred_element_type=F32)
    meta_out[...] = meta.reshape(nd, 1, 128)
    meta_in[nd - 1] = meta_out[nd - 1]

    own_load.wait()
    mine = hcols[...]
    self_at = (nd - 1) * SLOTS

    def gather(c):
        lo, hi = chunks[c]
        n = (hi - lo) * SLOTS
        pick = (iota((n, rows), 0) + lo * SLOTS == slot_across).astype(F32).astype(BF16)
        send[lo * SLOTS:hi * SLOTS] = jnp.dot(pick, mine, preferred_element_type=F32).astype(BF16)

    def issue(c):
        for i in range(*chunks[c]):
            if i < nd - 1:
                cut = pl.ds(i * SLOTS, SLOTS)
                pltpu.make_async_remote_copy(
                    send.at[cut], recv.at[cut], data_send.at[c], data_recv.at[c],
                    device_id=at(*spots[i]), device_id_type=MESH).start()

    def tell(c):
        lo, hi = chunks[c]
        for i in range(lo, min(hi, nd - 1)):
            pltpu.make_async_remote_copy(
                meta_out.at[i], meta_in.at[i], meta_send.at[c], meta_recv.at[c],
                device_id=at(*spots[i]), device_id_type=MESH).start()

    gather(0)
    pl.semaphore_wait(barrier, len(greeted) + ntp - 1)
    for dx in range(1, nx):
        pl.semaphore_signal(
            ready.at[nx - dx - 1], inc=1, device_id=at(dx, 0), device_id_type=MESH)
    tell(0)
    issue(0)
    unheard = set(range(1, nx))
    for c in range(1, len(chunks)):
        gather(c)
        for dx in sorted({dx for dx, dz in plan[c] if dz} & unheard):
            pl.semaphore_wait(ready.at[dx - 1], 1)
            unheard.remove(dx)
        tell(c)
        issue(c)
    recv[self_at:] = send[self_at:]

    loads = [
        pltpu.make_async_copy(down, dbuf, load_sem.at[1]),
        pltpu.make_async_copy(up, ubuf, load_sem.at[2]),
    ]
    for load in loads:
        load.start()
    nk = depth // own
    base_loads = []
    for k in range(nk):
        cut = pl.ds(k * own, own)
        base_loads.append((
            pltpu.make_async_copy(hidden.at[:, cut], hbuf.at[k], base_sem.at[0, k]),
            pltpu.make_async_copy(weight.at[cut], wbuf.at[k], base_sem.at[1, k]),
        ))
    for pair in base_loads:
        for load in pair:
            load.start()

    base = jnp.zeros((rows, out.shape[1]), F32)
    for k in range(nk):
        for load in base_loads[k]:
            load.wait()
        base = base + jnp.dot(hbuf[k], wbuf[k], preferred_element_type=F32)

    for load in loads:
        load.wait()

    def whole(ref, sem):
        return pltpu.make_async_copy(ref, ref, sem)

    def away(ref, c):
        lo, hi = chunks[c]
        return ref.at[pl.ds(lo * SLOTS, (min(hi, nd - 1) - lo) * SLOTS)]

    def told(ref, c):
        lo, hi = chunks[c]
        return ref.at[pl.ds(lo, min(hi, nd - 1) - lo)]

    def kept(c):
        lo, hi = chunks[c]
        n = (hi - lo) * SLOTS
        m = jnp.broadcast_to(meta_in[lo:hi], (hi - lo, SLOTS, 128)).reshape(n, 128)
        hit = iota((n, 128), 1) == iota((n, 128), 0) % SLOTS
        m = jnp.sum(jnp.where(hit, m, 0.0), axis=1, keepdims=True)
        return iota((n, members * RANK), 1) // RANK == m.astype(jnp.int32)

    def halves(c):
        lo, hi = chunks[c]
        half = (hi - lo) * SLOTS // 2
        return half, lo * SLOTS // 2

    def project(c):
        lo, hi = chunks[c]
        half, first = halves(c)
        whole(told(meta_in, c), meta_recv.at[c]).wait()
        keep = kept(c)
        whole(away(recv, c), data_recv.at[c]).wait()
        scores = jnp.dot(recv[lo * SLOTS:hi * SLOTS], dbuf[...], preferred_element_type=F32)
        scores = jnp.where(keep, scores, 0.0)
        total = scores[:, :128]
        for j in range(1, members * RANK // 128):
            total = total + scores[:, j * 128:(j + 1) * 128]
        total = total + pltpu.roll(total, RANK, 1)
        packed = jnp.where(iota((half, 128), 1) < RANK, total[:half], total[half:])
        part[first:first + half] = packed.astype(BF16)
        for o in sorted(range(1, ntp), key=lambda o: -min(o, ntp - o)):
            pltpu.make_async_remote_copy(
                part.at[pl.ds(first, half)],
                parts.at[pl.ds(first * (ntp - 1) + (o - 1) * half, half)],
                part_send.at[c], part_recv.at[c],
                device_id=peer(o), device_id_type=MESH).start()
        return packed, keep

    def landed(c):
        half, first = halves(c)
        return parts.at[pl.ds(first * (ntp - 1), half * (ntp - 1))]

    def raise_up(c, packed, keep):
        lo, hi = chunks[c]
        half, first = halves(c)
        whole(landed(c), part_recv.at[c]).wait()
        total = packed
        for o in range(ntp - 1):
            start = first * (ntp - 1) + o * half
            total = total + parts[start:start + half].astype(F32)
        turned = pltpu.roll(total, RANK, 1)
        left = iota((half, 128), 1) < RANK
        both = jnp.concatenate(
            [jnp.where(left, total, turned), jnp.where(left, turned, total)], axis=0)
        spread = jnp.concatenate([both] * (members * RANK // 128), axis=1)
        spread = jnp.where(keep, spread, 0.0).astype(BF16)
        yout[lo * SLOTS:hi * SLOTS] = jnp.dot(
            spread, ubuf[...], preferred_element_type=F32).astype(BF16)
        for i in range(lo, hi):
            cut = pl.ds(i * SLOTS, SLOTS)
            if i < nd - 1:
                dx, dz = spots[i]
                pltpu.make_async_remote_copy(
                    yout.at[cut], yin.at[cut], ret_send.at[c], ret_recv.at[c],
                    device_id=at(-dx, -dz), device_id_type=MESH).start()
            else:
                yin[self_at:] = yout[self_at:]

    held = [project(c) for c in range(len(chunks))]
    for c, kept_ranks in enumerate(held):
        raise_up(c, *kept_ranks)

    delta = base
    for c, (lo, hi) in enumerate(chunks):
        n = (hi - lo) * SLOTS
        pick = (iota((rows, n), 1) + lo * SLOTS == slot_down).astype(F32).astype(BF16)
        whole(away(yin, c), ret_recv.at[c]).wait()
        delta = delta + jnp.dot(pick, yin[lo * SLOTS:hi * SLOTS], preferred_element_type=F32)
    out[...] = delta.astype(BF16)

    for c in range(len(chunks)):
        whole(told(meta_out, c), meta_send.at[c]).wait()
        whole(away(send, c), data_send.at[c]).wait()
        whole(away(yout, c), ret_send.at[c]).wait()
        whole(landed(c), part_send.at[c]).wait()


def build(mesh, nx, nz, plan):
    ntp = mesh.shape["tp"]

    def step(hidden, weight, group, member, down, up):
        rows, depth = hidden.shape
        own, ranks = down.shape
        features = weight.shape[1]
        nk = depth // own
        nd = nx * nz
        total = nd * SLOTS
        nc = len(plan)
        vmem = pl.BlockSpec(memory_space=pltpu.VMEM)
        hbm = pl.BlockSpec(memory_space=pl.ANY)
        dma = pltpu.SemaphoreType.DMA
        return pl.pallas_call(
            functools.partial(kernel, nx, nz, ntp, plan),
            out_shape=pltpu.VMEM((rows, features), BF16),
            in_specs=[hbm, hbm, vmem, vmem, hbm, hbm],
            out_specs=vmem,
            scratch_shapes=[
                pltpu.VMEM((rows, own), BF16),
                pltpu.VMEM((nk, rows, own), BF16),
                pltpu.VMEM((nk, own, features), BF16),
                pltpu.VMEM((own, ranks), BF16),
                pltpu.VMEM((ranks, features), BF16),
                pltpu.VMEM((total, own), BF16),
                pltpu.VMEM((total, own), BF16),
                pltpu.VMEM((nd, 1, 128), F32),
                pltpu.VMEM((nd, 1, 128), F32),
                pltpu.VMEM((total // 2, 128), BF16),
                pltpu.VMEM(((ntp - 1) * total // 2, 128), BF16),
                pltpu.VMEM((total, features), BF16),
                pltpu.VMEM((total, features), BF16),
                dma((3,)), dma((2, nk)), dma((nc,)), dma((nc,)), dma((nc,)), dma((nc,)),
                dma((nc,)), dma((nc,)), dma((nc,)), dma((nc,)),
                pltpu.SemaphoreType.REGULAR((nx - 1,)),
            ],
            compiler_params=pltpu.CompilerParams(
                collective_id=0, has_side_effects=True, vmem_limit_bytes=56 * 1024 * 1024
            ),
        )(hidden, weight, group.reshape(1, rows), member.reshape(1, rows), down, up)

    placed = (P("ad", None), P(None, "tp"), P("ad", None), P("ad"), P("tp", "ad"), P("ad", "tp"))
    return jax.shard_map(
        step, mesh=mesh, in_specs=placed, out_specs=P("ad", "tp"), check_vma=False
    )


def plan():
    far = (4, 3, 5, 2, 6, 1, 7)
    spots = [(0, dz) for dz in far[:3]] + [(2, 0), (1, 0), (3, 0)]
    spots += [(2, dz) for dz in far] + [(dx, dz) for dz in far for dx in (1, 3)]
    spots += [(0, dz) for dz in far[3:]] + [(0, 0)]
    ends = (6, 14, 20, 26, 32)
    return [spots[lo:hi] for lo, hi in zip((0,) + ends, ends)]


def solution(mesh):
    return build(mesh, 4, 8, plan())
```

```python
import functools

import jax
import jax.numpy as jnp
from jax import lax
from jax.experimental import pallas as pl
from jax.experimental.pallas import tpu as pltpu
from jax.sharding import PartitionSpec as P

RANK = 64
SLOTS = 16
F32 = jnp.float32
BF16 = jnp.bfloat16
MESH = pl.DeviceIdType.MESH


def iota(shape, axis):
    return lax.broadcasted_iota(jnp.int32, shape, axis)


def kernel(
    nx, nz, ntp, plan, hidden, weight, group, member, down, up, out,
    hcols, hbuf, wbuf, dbuf, ubuf, send, recv, meta_out, meta_in,
    part, parts, yout, yin,
    load_sem, base_sem, data_send, data_recv, meta_send, meta_recv,
    part_send, part_recv, ret_send, ret_recv, ready,
):
    rows, depth = hidden.shape
    own = hcols.shape[1]
    members = dbuf.shape[1] // RANK
    ad = lax.axis_index("ad")
    tp = lax.axis_index("tp")
    x, z = ad // nz, lax.rem(ad, nz)

    def at(dx, dz):
        return {"ad": lax.rem(x + dx + nx, nx) * nz + lax.rem(z + dz + nz, nz)}

    def peer(o):
        return {"tp": lax.rem(tp + o, ntp)}

    spots = [spot for chunk in plan for spot in chunk]
    chunks, nd = [], 0
    for chunk in plan:
        chunks.append((nd, nd + len(chunk)))
        nd += len(chunk)
    offsets = spots[:-1]
    first = pl.multiple_of(tp * own, own)
    own_load = pltpu.make_async_copy(hidden.at[:, pl.ds(first, own)], hcols, load_sem.at[0])
    own_load.start()

    barrier = pltpu.get_barrier_semaphore()
    greeted = [(0, dz) for dz in range(1, nz)] + [(dx, 0) for dx in range(1, nx)]
    for dx, dz in greeted:
        pl.semaphore_signal(barrier, inc=1, device_id=at(dx, dz), device_id_type=MESH)
    for o in range(1, ntp):
        pl.semaphore_signal(barrier, inc=1, device_id=peer(o), device_id_type=MESH)

    goes = group[...]
    gx, gz = goes // nz, goes % nz

    code = (gx - x + nx) % nx * nz + (gz - z + nz) % nz
    rel = jnp.zeros_like(code)
    for i, (dx, dz) in enumerate(spots):
        rel = jnp.where(code == dx * nz + dz, i, rel)
    rel_across = rel.astype(F32)
    square = (rows, rows)
    down_at, across_at = iota(square, 0), iota(square, 1)
    rel_down = jnp.sum(jnp.where(down_at == across_at, rel_across, 0.0), axis=1, keepdims=True)
    same = (rel_down == rel_across).astype(F32)
    k_across = jnp.sum(jnp.where(down_at < across_at, same, 0.0), axis=0, keepdims=True)
    k_down = jnp.sum(jnp.where(across_at < down_at, same, 0.0), axis=1, keepdims=True)
    slot_across = (rel_across * SLOTS + k_across).astype(jnp.int32)
    slot_down = (rel_down * SLOTS + k_down).astype(jnp.int32)
    named = jnp.where(
        iota((nd, rows), 0) == rel_across.astype(jnp.int32), member[...].astype(F32), 0.0
    ).astype(BF16)
    placed = (iota((rows, 128), 1) == k_down.astype(jnp.int32)).astype(F32).astype(BF16)
    meta = jnp.dot(named, placed, preferred_element_type=F32)
    meta_out[...] = meta.reshape(nd, 1, 128)
    meta_in[nd - 1] = meta_out[nd - 1]

    own_load.wait()
    mine = hcols[...]
    self_at = (nd - 1) * SLOTS

    def gather(c):
        lo, hi = chunks[c]
        n = (hi - lo) * SLOTS
        pick = (iota((n, rows), 0) + lo * SLOTS == slot_across).astype(F32).astype(BF16)
        send[lo * SLOTS:hi * SLOTS] = jnp.dot(pick, mine, preferred_element_type=F32).astype(BF16)

    def issue(c):
        for i in range(*chunks[c]):
            if i < nd - 1:
                cut = pl.ds(i * SLOTS, SLOTS)
                pltpu.make_async_remote_copy(
                    send.at[cut], recv.at[cut], data_send.at[c], data_recv.at[c],
                    device_id=at(*spots[i]), device_id_type=MESH).start()

    def tell(c):
        lo, hi = chunks[c]
        for i in range(lo, min(hi, nd - 1)):
            pltpu.make_async_remote_copy(
                meta_out.at[i], meta_in.at[i], meta_send.at[c], meta_recv.at[c],
                device_id=at(*spots[i]), device_id_type=MESH).start()

    gather(0)
    pl.semaphore_wait(barrier, len(greeted) + ntp - 1)
    for dx in range(1, nx):
        pl.semaphore_signal(
            ready.at[nx - dx - 1], inc=1, device_id=at(dx, 0), device_id_type=MESH)
    tell(0)
    issue(0)
    unheard = set(range(1, nx))
    for c in range(1, len(chunks)):
        gather(c)
        for dx in sorted({dx for dx, dz in plan[c] if dz} & unheard):
            pl.semaphore_wait(ready.at[dx - 1], 1)
            unheard.remove(dx)
        tell(c)
        issue(c)
    recv[self_at:] = send[self_at:]

    loads = [
        pltpu.make_async_copy(down, dbuf, load_sem.at[1]),
        pltpu.make_async_copy(up, ubuf, load_sem.at[2]),
    ]
    for load in loads:
        load.start()
    nk = depth // own
    base_loads = []
    for k in range(nk):
        cut = pl.ds(k * own, own)
        base_loads.append((
            pltpu.make_async_copy(hidden.at[:, cut], hbuf.at[k], base_sem.at[0, k]),
            pltpu.make_async_copy(weight.at[cut], wbuf.at[k], base_sem.at[1, k]),
        ))
    for pair in base_loads:
        for load in pair:
            load.start()

    base = jnp.zeros((rows, out.shape[1]), F32)
    for k in range(nk):
        for load in base_loads[k]:
            load.wait()
        base = base + jnp.dot(hbuf[k], wbuf[k], preferred_element_type=F32)

    for load in loads:
        load.wait()

    def whole(ref, sem):
        return pltpu.make_async_copy(ref, ref, sem)

    def away(ref, c):
        lo, hi = chunks[c]
        return ref.at[pl.ds(lo * SLOTS, (min(hi, nd - 1) - lo) * SLOTS)]

    def told(ref, c):
        lo, hi = chunks[c]
        return ref.at[pl.ds(lo, min(hi, nd - 1) - lo)]

    def kept(c):
        lo, hi = chunks[c]
        n = (hi - lo) * SLOTS
        m = jnp.broadcast_to(meta_in[lo:hi], (hi - lo, SLOTS, 128)).reshape(n, 128)
        hit = iota((n, 128), 1) == iota((n, 128), 0) % SLOTS
        m = jnp.sum(jnp.where(hit, m, 0.0), axis=1, keepdims=True)
        return iota((n, members * RANK), 1) // RANK == m.astype(jnp.int32)

    def halves(c):
        lo, hi = chunks[c]
        half = (hi - lo) * SLOTS // 2
        return half, lo * SLOTS // 2

    def project(c):
        lo, hi = chunks[c]
        half, first = halves(c)
        whole(told(meta_in, c), meta_recv.at[c]).wait()
        keep = kept(c)
        whole(away(recv, c), data_recv.at[c]).wait()
        scores = jnp.dot(recv[lo * SLOTS:hi * SLOTS], dbuf[...], preferred_element_type=F32)
        scores = jnp.where(keep, scores, 0.0)
        total = scores[:, :128]
        for j in range(1, members * RANK // 128):
            total = total + scores[:, j * 128:(j + 1) * 128]
        total = total + pltpu.roll(total, RANK, 1)
        packed = jnp.where(iota((half, 128), 1) < RANK, total[:half], total[half:])
        part[first:first + half] = packed.astype(BF16)
        for o in sorted(range(1, ntp), key=lambda o: -min(o, ntp - o)):
            pltpu.make_async_remote_copy(
                part.at[pl.ds(first, half)],
                parts.at[pl.ds(first * (ntp - 1) + (o - 1) * half, half)],
                part_send.at[c], part_recv.at[c],
                device_id=peer(o), device_id_type=MESH).start()
        return packed, keep

    def landed(c):
        half, first = halves(c)
        return parts.at[pl.ds(first * (ntp - 1), half * (ntp - 1))]

    def raise_up(c, packed, keep):
        lo, hi = chunks[c]
        half, first = halves(c)
        whole(landed(c), part_recv.at[c]).wait()
        total = packed
        for o in range(ntp - 1):
            start = first * (ntp - 1) + o * half
            total = total + parts[start:start + half].astype(F32)
        turned = pltpu.roll(total, RANK, 1)
        left = iota((half, 128), 1) < RANK
        both = jnp.concatenate(
            [jnp.where(left, total, turned), jnp.where(left, turned, total)], axis=0)
        spread = jnp.concatenate([both] * (members * RANK // 128), axis=1)
        spread = jnp.where(keep, spread, 0.0).astype(BF16)
        yout[lo * SLOTS:hi * SLOTS] = jnp.dot(
            spread, ubuf[...], preferred_element_type=F32).astype(BF16)
        for i in range(lo, hi):
            cut = pl.ds(i * SLOTS, SLOTS)
            if i < nd - 1:
                dx, dz = spots[i]
                pltpu.make_async_remote_copy(
                    yout.at[cut], yin.at[cut], ret_send.at[c], ret_recv.at[c],
                    device_id=at(-dx, -dz), device_id_type=MESH).start()
            else:
                yin[self_at:] = yout[self_at:]

    held = [project(c) for c in range(len(chunks))]
    for c, kept_ranks in enumerate(held):
        raise_up(c, *kept_ranks)

    delta = base
    for c, (lo, hi) in enumerate(chunks):
        n = (hi - lo) * SLOTS
        pick = (iota((rows, n), 1) + lo * SLOTS == slot_down).astype(F32).astype(BF16)
        whole(away(yin, c), ret_recv.at[c]).wait()
        delta = delta + jnp.dot(pick, yin[lo * SLOTS:hi * SLOTS], preferred_element_type=F32)
    out[...] = delta.astype(BF16)

    for c in range(len(chunks)):
        whole(told(meta_out, c), meta_send.at[c]).wait()
        whole(away(send, c), data_send.at[c]).wait()
        whole(away(yout, c), ret_send.at[c]).wait()
        whole(landed(c), part_send.at[c]).wait()


def build(mesh, nx, nz, plan):
    ntp = mesh.shape["tp"]

    def step(hidden, weight, group, member, down, up):
        rows, depth = hidden.shape
        own, ranks = down.shape
        features = weight.shape[1]
        nk = depth // own
        nd = nx * nz
        total = nd * SLOTS
        nc = len(plan)
        vmem = pl.BlockSpec(memory_space=pltpu.VMEM)
        hbm = pl.BlockSpec(memory_space=pl.ANY)
        dma = pltpu.SemaphoreType.DMA
        return pl.pallas_call(
            functools.partial(kernel, nx, nz, ntp, plan),
            out_shape=pltpu.VMEM((rows, features), BF16),
            in_specs=[hbm, hbm, vmem, vmem, hbm, hbm],
            out_specs=vmem,
            scratch_shapes=[
                pltpu.VMEM((rows, own), BF16),
                pltpu.VMEM((nk, rows, own), BF16),
                pltpu.VMEM((nk, own, features), BF16),
                pltpu.VMEM((own, ranks), BF16),
                pltpu.VMEM((ranks, features), BF16),
                pltpu.VMEM((total, own), BF16),
                pltpu.VMEM((total, own), BF16),
                pltpu.VMEM((nd, 1, 128), F32),
                pltpu.VMEM((nd, 1, 128), F32),
                pltpu.VMEM((total // 2, 128), BF16),
                pltpu.VMEM(((ntp - 1) * total // 2, 128), BF16),
                pltpu.VMEM((total, features), BF16),
                pltpu.VMEM((total, features), BF16),
                dma((3,)), dma((2, nk)), dma((nc,)), dma((nc,)), dma((nc,)), dma((nc,)),
                dma((nc,)), dma((nc,)), dma((nc,)), dma((nc,)),
                pltpu.SemaphoreType.REGULAR((nx - 1,)),
            ],
            compiler_params=pltpu.CompilerParams(
                collective_id=0, has_side_effects=True, vmem_limit_bytes=56 * 1024 * 1024
            ),
        )(hidden, weight, group.reshape(1, rows), member.reshape(1, rows), down, up)

    placed = (P("ad", None), P(None, "tp"), P("ad", None), P("ad"), P("tp", "ad"), P("ad", "tp"))
    return jax.shard_map(
        step, mesh=mesh, in_specs=placed, out_specs=P("ad", "tp"), check_vma=False
    )


def plan():
    far = (4, 3, 5, 2, 6, 1, 7)
    spots = [(0, dz) for dz in far[:3]] + [(2, 0), (1, 0), (3, 0)]
    spots += [(2, dz) for dz in far] + [(dx, dz) for dz in far for dx in (1, 3)]
    spots += [(0, dz) for dz in far[3:]] + [(0, 0)]
    ends = (6, 14, 20, 26, 30, 32)
    return [spots[lo:hi] for lo, hi in zip((0,) + ends, ends)]


def solution(mesh):
    return build(mesh, 4, 8, plan())
```
